32 devices in a mesh: seq: 4 (over y, core), strand: 2 (over x), head: 4 (over z).
Axes of the slice: x: 2, y: 2, z: 4, core: 2. Of those that a mesh axis runs over, the one named last changes fastest.
Arguments:
- top: bfloat16 [4, 2, 1024, 1536], P('head', 'strand', 'seq'), may hold values from -6 to 6
- grad_heads: bfloat16 [4, 2, 1024, 1536], P(None, 'strand', 'seq', 'head'), may hold values from -6 to 6
- tap_weight_grid: bfloat16 [3, 768, 768], P(None, 'seq'), may hold values from -0.125 to 0.125
- out_w: bfloat16 [768, 768], P('seq'), may hold values from -0.21875 to 0.21875
- mix_w: bfloat16 [768, 768], P('seq'), may hold values from -0.21875 to 0.21875
- rc_perm: int32 [768], replicated, may hold values from 0 to 767, each once
Outputs:
- restored: bfloat16 [4, 2, 1024, 1536], P('head', 'strand', 'seq')
- grad_input: bfloat16 [4, 2, 1024, 1536], P('head', 'strand', 'seq')
The draws below stay inside these ranges and needn't reach their ends.
Inputs may be any that keep to these rules, and one draw needn't show every extreme that they name: `rc_perm`: every channel index appears exactly once.
All inputs are finite; a program needn't handle non-finite values.
Results may differ from the reference program's by a relative error of at most 0.008.
Values may be sent and summed in bfloat16 or wider, within the bound.
A program may use at most 64 MiB of HBM per device.

```python
import jax
import jax.numpy as jnp

C = 1536
HALF = 768
INNER = 768
DILATION_STEP = 128
SAMPLES = 4
POS = 1024


def block_scale(own_key, extent, cuts, smallest, top_value):
    level, own = 1.0, jax.random.fold_in(own_key, 6)
    for axis_at, blocks in cuts:
        heights = jnp.exp(jax.random.uniform(jax.random.fold_in(own, axis_at), (blocks,), jnp.float32, smallest / len(cuts), top_value / len(cuts)))
        level = level * jnp.repeat(heights, extent[axis_at] // blocks).reshape([-1 if axis == axis_at else 1 for axis in range(len(extent))])
    return level


def scatter_about(own_key, extent, deviation, most, pieces=(), kind=jnp.bfloat16):
    entries = jax.random.normal(own_key, extent, jnp.float32) * deviation
    if len(pieces) > 0:
        entries = block_scale(own_key, extent, pieces, -0.22, 0.18) * entries
    return jnp.clip(entries, min=-most, max=most).astype(kind)


def setup_inputs(seed: int = 0) -> dict:
    streams_of = jax.random.split(jax.random.key(seed), 7)
    return {
        "top": scatter_about(streams_of[0], (SAMPLES, 2, POS, C), 1.0, 6.0, ((0, 4), (1, 2), (2, 4))),
        "grad_heads": scatter_about(streams_of[1], (SAMPLES, 2, POS, C), 1.0, 6.0, ((1, 2), (2, 4), (3, 4))),
        "tap_weight_grid": scatter_about(streams_of[2], (3, HALF, INNER), (3 * HALF) ** -0.5, 0.125, ((1, 4),)),
        "out_w": scatter_about(streams_of[3], (INNER, HALF), INNER ** -0.5, 0.21875, ((0, 4),)),
        "mix_w": scatter_about(streams_of[4], (HALF, HALF), HALF ** -0.5, 0.21875, ((0, 4),)),
        "rc_perm": jax.random.permutation(streams_of[5], HALF).astype(jnp.int32),
    }


def product(left, right):
    return jnp.einsum('spc,cd->spd', left.astype(jnp.float32), right.astype(jnp.float32))

def dilated_result(field, kernel, dilation):
    length = field.shape[1]
    padded = jnp.pad(field, ((0, 0), (dilation, dilation), (0, 0)))
    total = jnp.zeros((field.shape[0], length, kernel.shape[2]), jnp.float32)
    for offset in range(3):
        window = padded[:, offset * dilation:offset * dilation + length]
        total = total + product(window, kernel[offset])
    return total

def transposed_result(grad, kernel, dilation):
    length = grad.shape[1]
    padded = jnp.pad(grad, ((0, 0), (dilation, dilation), (0, 0)))
    total = jnp.zeros((grad.shape[0], length, kernel.shape[1]), jnp.float32)
    for offset in range(3):
        start = (2 - offset) * dilation
        window = padded[:, start:start + length]
        total = total + product(window, kernel[offset].T)
    return total

def one_sample(top, grads, tap_weight_grid, out_w, mix_w, rc_perm, inverse):
    top_a = top[..., :HALF]
    top_b = top[..., HALF:]
    mirror = jnp.take(top_a[::-1], rc_perm, axis=2)
    paired = (top_a.astype(jnp.float32) + mirror.astype(jnp.float32)).astype(jnp.bfloat16)
    second_input = (top_b.astype(jnp.float32) - product(paired, mix_w)).astype(jnp.bfloat16)
    preactivation_rows = dilated_result(second_input, tap_weight_grid, DILATION_STEP)
    hidden = jax.nn.gelu(preactivation_rows).astype(jnp.bfloat16)
    input_a = (top_a.astype(jnp.float32) - product(hidden, out_w)).astype(jnp.bfloat16)
    grad_a = grads[..., :HALF]
    second_gradient = grads[..., HALF:]
    backed = product(second_gradient, mix_w.T).astype(jnp.bfloat16)
    returned = jnp.take(backed, inverse, axis=2)[::-1]
    cot_a = (grad_a.astype(jnp.float32) + backed.astype(jnp.float32) + returned.astype(jnp.float32)).astype(jnp.bfloat16)
    pulled = product(cot_a, out_w.T)
    unused, slope = jax.vjp(jax.nn.gelu, preactivation_rows)
    preactivation_cotangent = slope(pulled)[0].astype(jnp.bfloat16)
    cotangent_second = (second_gradient.astype(jnp.float32) + transposed_result(preactivation_cotangent, tap_weight_grid, DILATION_STEP)).astype(jnp.bfloat16)
    return (jnp.concatenate([input_a, second_input], axis=2), jnp.concatenate([cot_a, cotangent_second], axis=2))

def reference(top, grad_heads, tap_weight_grid, out_w, mix_w, rc_perm):
    inverse = jnp.zeros((HALF,), jnp.int32).at[rc_perm].set(jnp.arange(HALF, dtype=jnp.int32))
    restored_list = []
    grad_list = []
    for sample in range(SAMPLES):
        restored_one, grad_one = one_sample(top[sample], grad_heads[sample], tap_weight_grid, out_w, mix_w, rc_perm, inverse)
        restored_list.append(restored_one)
        grad_list.append(grad_one)
    return (jnp.stack(restored_list), jnp.stack(grad_list))
```

```python
import functools
import math

import jax
import jax.numpy as jnp
from jax import lax
from jax.experimental import pallas as pl
from jax.experimental.pallas import tpu as pltpu
from jax.sharding import PartitionSpec as P

MESH = pl.DeviceIdType.MESH
F32, BF16 = jnp.float32, jnp.bfloat16
ROUTES = ("far", "strand", "head", "head", "head")


def dot(a, b):
    return jnp.dot(a, b, preferred_element_type=F32)


def dot_t(a, b):
    return lax.dot_general(a, b, (((1,), (1,)), ((), ())), preferred_element_type=F32)


def kernel(
    n, heads, relay,
    top, grad, taps, out_w, mix_w, perm,
    restored, grad_in,
    full, onehot, topv, other, paired, cot, pad, padc, backed, back_in, pre, pulled, rest, gout,
    send, recv, local,
):
    s, x, z = lax.axis_index("seq"), lax.axis_index("strand"), lax.axis_index("head")
    length, half = other.shape
    dil = length // 2
    rows, width = mix_w.shape[0], grad.shape[3]
    started, counter, waits = [], [0], [0]

    def remote(src, dst, device):
        i = counter[0]
        counter[0] += 1
        return lambda s_ref=src, d_ref=dst: pltpu.make_async_remote_copy(
            src_ref=s_ref, dst_ref=d_ref, send_sem=send.at[i], recv_sem=recv.at[i],
            device_id=device, device_id_type=MESH)

    def start(make):
        copy = make()
        copy.start()
        started.append(copy)

    def arrived(make, ref):
        make(ref, ref).wait_recv()

    def here(src, dst):
        copy = pltpu.make_async_copy(src, dst, local.at[waits[0]])
        waits[0] += 1
        copy.start()
        return copy

    weights = [mix_w, out_w] + [taps.at[k] for k in range(taps.shape[0])]
    count = len(weights)
    top_copy = here(top.at[0, 0], topv)
    own_z = here(grad.at[z, 0], cot.at[:, pl.ds(pl.multiple_of(z * width, 128), width)])
    if relay:
        base = pl.multiple_of(s * rows, 16)
        own_w = [here(w, full.at[m, pl.ds(base, rows), :]) for m, w in enumerate(weights)]
    else:
        own_w = [here(w, full.at[m]) for m, w in enumerate(weights)]

    barrier = pltpu.get_barrier_semaphore()
    ring = range(1, n) if relay else ((1, n - 1) if n > 2 else range(1, n))
    greeted = [{"seq": lax.rem(s + i, n)} for i in ring]
    greeted += [{"strand": 1 - x}] + [{"head": lax.rem(z + i, heads)} for i in range(1, heads)]
    for device in greeted:
        pl.semaphore_signal(barrier, inc=1, device_id=device, device_id_type=MESH)
    pl.semaphore_wait(barrier, len(greeted))

    to_strand = {"strand": 1 - x}
    swap = remote(top.at[0, 0, :, pl.ds(0, half)], other, to_strand)
    start(swap)

    if relay:
        core = lax.rem(s, 2)
        sib, far = s + 1 - 2 * core, lax.rem(s + 2, n)
        sib_far = lax.rem(sib + 2, n)
        hr = rows // 2

        def seg(m, owner, first, size):
            return full.at[m, pl.ds(pl.multiple_of(owner * rows + first, 16), size), :]

        plans = []
        for m in range(count):
            turn = {"far": None, "strand": x, "head": lax.rem(z, 2)}[ROUTES[m]]
            first, size = (0, rows) if turn is None else (pl.multiple_of(turn * hr, 16), hr)
            rest_first = None if turn is None else pl.multiple_of((1 - turn) * hr, 16)
            partner = {"far": None, "strand": to_strand, "head": {"head": z + 1 - 2 * lax.rem(z, 2)}}[ROUTES[m]]
            w = weights[m]
            plan = {
                "first": first, "size": size, "rest": rest_first,
                "sib": remote(w, seg(m, s, 0, rows), {"seq": sib}),
                "far": remote(w.at[pl.ds(first, size), :], seg(m, s, first, size), {"seq": far}),
                "fwd": remote(seg(m, far, first, size), seg(m, far, first, size), {"seq": sib}),
            }
            if turn is not None:
                plan["relay"] = remote(seg(m, far, first, size), seg(m, far, first, size), partner)
                plan["fwd2"] = remote(seg(m, far, rest_first, hr), seg(m, far, rest_first, hr), {"seq": sib})
            plans.append(plan)

    def push(m):
        if relay:
            start(plans[m]["far"])
            start(plans[m]["sib"])

    def stage_a(m):
        if relay:
            p = plans[m]
            arrived(p["far"], seg(m, far, p["first"], p["size"]))
            if p["rest"] is not None:
                start(p["relay"])
            start(p["fwd"])

    def stage_b(m):
        if relay and plans[m]["rest"] is not None:
            p = plans[m]
            arrived(p["relay"], seg(m, far, p["rest"], hr))
            start(p["fwd2"])

    def stage_c(m):
        own_w[m].wait()
        if relay:
            p = plans[m]
            arrived(p["sib"], seg(m, sib, 0, rows))
            arrived(p["fwd"], seg(m, sib_far, p["first"], p["size"]))
            if p["rest"] is not None:
                arrived(p["fwd2"], seg(m, sib_far, p["rest"], hr))

    def piece(h, owner):
        return cot.at[pl.ds(h * dil, dil), pl.ds(pl.multiple_of(owner * width, 128), width)]

    gifts = []
    for h in range(2):
        gifts.append([
            remote(grad.at[lax.rem(z + i, heads), 0, pl.ds(h * dil, dil), :], piece(h, z),
                   {"head": lax.rem(z + i, heads)})
            for i in range(1, heads)])
    push(0)
    for make in gifts[0]:
        start(make)
    for m in range(1, count):
        push(m)
    for make in gifts[1]:
        start(make)

    index = lax.broadcasted_iota(jnp.int32, (half, half), 0)
    onehot[...] = jnp.where(index == perm[...], 1.0, 0.0).astype(BF16)

    @pl.when(s == 0)
    def _():
        pad[0:dil] = jnp.zeros((dil, half), BF16)
        padc[0:dil] = jnp.zeros((dil, half), BF16)

    @pl.when(s == n - 1)
    def _():
        pad[3 * dil:] = jnp.zeros((dil, half), BF16)
        padc[3 * dil:] = jnp.zeros((dil, half), BF16)

    top_copy.wait()
    arrived(swap, other)
    paired[...] = (topv[:, :half].astype(F32) + dot(other[...], onehot[...])).astype(BF16)

    def halo(buf):
        up = remote(buf.at[pl.ds(2 * dil, dil)], buf.at[pl.ds(0, dil)], {"seq": lax.rem(s + 1, n)})
        down = remote(buf.at[pl.ds(dil, dil)], buf.at[pl.ds(3 * dil, dil)], {"seq": lax.rem(s + n - 1, n)})

        @pl.when(s < n - 1)
        def _():
            up().start()

        @pl.when(s > 0)
        def _():
            down().start()

        def finish():
            @pl.when(s > 0)
            def _():
                arrived(up, buf.at[pl.ds(0, dil)])
                down().wait_send()

            @pl.when(s < n - 1)
            def _():
                arrived(down, buf.at[pl.ds(3 * dil, dil)])
                up().wait_send()

        return finish

    returns = [remote(backed.at[pl.ds(h * dil, dil)], back_in.at[pl.ds(h * dil, dil)], to_strand)
               for h in range(2)]

    def back(h):
        if h == 0:
            own_z.wait()
        for i in range(1, heads):
            arrived(gifts[h][i - 1], piece(h, lax.rem(z + heads - i, heads)))
        rows_h = slice(h * dil, (h + 1) * dil)
        backed[rows_h] = dot_t(cot[rows_h, half:], full[0]).astype(BF16)
        start(returns[h])

    stage_a(0)
    stage_a(1)
    stage_b(0)
    stage_c(0)
    input_b = (topv[:, half:].astype(F32) - dot(paired[...], full[0])).astype(BF16)
    pad[dil:3 * dil] = input_b
    rest[:, half:] = input_b
    halo_b = halo(pad)
    stores = [here(rest.at[:, pl.ds(half, half)], restored.at[0, 0, :, pl.ds(half, half)])]
    back(0)
    stage_a(2)
    stage_b(1)
    stage_c(1)
    halo_b()
    stage_a(3)
    stage_b(2)
    stage_c(2)
    pre[...] = dot(pad[0:2 * dil], full[2])
    back(1)
    stage_a(4)
    stage_b(3)
    stage_c(3)
    pre[...] += dot(pad[dil:3 * dil], full[3])

    for h in range(2):
        rows_h = slice(h * dil, (h + 1) * dil)
        arrived(returns[h], back_in.at[pl.ds(h * dil, dil)])
        returned = dot_t(back_in[rows_h], onehot[...])
        cot_a = (cot[rows_h, :half].astype(F32) + backed[rows_h].astype(F32) + returned).astype(BF16)
        gout[rows_h, :half] = cot_a
        pulled[rows_h] = dot_t(cot_a, full[1])
    stores.append(here(gout.at[:, pl.ds(0, half)], grad_in.at[0, 0, :, pl.ds(0, half)]))

    stage_b(4)
    stage_c(4)
    scale = math.sqrt(2.0 / math.pi)
    for h in range(2):
        rows_h = slice(h * dil, (h + 1) * dil)
        v = pre[rows_h] + dot(pad[(2 + h) * dil:(3 + h) * dil], full[4])
        square = v * v
        t = jnp.tanh(scale * (v + 0.044715 * (square * v)))
        cdf = 0.5 * (1.0 + t)
        slope = cdf + 0.5 * v * (1.0 - t * t) * (scale * (1.0 + 3 * 0.044715 * square))
        padc[(1 + h) * dil:(2 + h) * dil] = (pulled[rows_h] * slope).astype(BF16)
        paired[rows_h] = (v * cdf).astype(BF16)
    halo_c = halo(padc)
    rest[:, :half] = (topv[:, :half].astype(F32) - dot(paired[...], full[1])).astype(BF16)
    stores.append(here(rest.at[:, pl.ds(0, half)], restored.at[0, 0, :, pl.ds(0, half)]))
    total = cot[:, half:].astype(F32) + dot_t(padc[dil:3 * dil], full[3])
    low = total[:dil] + dot_t(padc[2 * dil:3 * dil], full[2])
    high = total[dil:] + dot_t(padc[dil:2 * dil], full[4])
    halo_c()
    gout[:dil, half:] = (low + dot_t(padc[:dil], full[4])).astype(BF16)
    gout[dil:, half:] = (high + dot_t(padc[3 * dil:], full[2])).astype(BF16)
    stores.append(here(gout.at[:, pl.ds(half, half)], grad_in.at[0, 0, :, pl.ds(half, half)]))
    for copy in started:
        copy.wait_send()
    for copy in stores:
        copy.wait()


def solution(mesh):
    n, heads = mesh.shape["seq"], mesh.shape["head"]

    def shards(top, grad, taps, out_w, mix_w, rc_perm):
        relay = n == 4 and heads % 2 == 0 and mix_w.shape[0] % 32 == 0
        if not relay:
            taps = lax.all_gather(taps, "seq", axis=1, tiled=True)
            out_w = lax.all_gather(out_w, "seq", axis=0, tiled=True)
            mix_w = lax.all_gather(mix_w, "seq", axis=0, tiled=True)
        length, half = top.shape[2], top.shape[3] // 2
        block = (length, half)
        copies = 1 + 5 * (taps.shape[0] + 2) + 2 * (heads - 1) + 6
        return pl.pallas_call(
            functools.partial(kernel, n, heads, relay),
            out_shape=[jax.ShapeDtypeStruct(top.shape, BF16)] * 2,
            in_specs=[pl.BlockSpec(memory_space=pl.ANY)] * 5 + [pl.BlockSpec(memory_space=pltpu.VMEM)],
            out_specs=[pl.BlockSpec(memory_space=pl.ANY)] * 2,
            scratch_shapes=[
                pltpu.VMEM((taps.shape[0] + 2, half, half), BF16),
                pltpu.VMEM((half, half), BF16),
                pltpu.VMEM((length, 2 * half), BF16),
                pltpu.VMEM(block, BF16),
                pltpu.VMEM(block, BF16),
                pltpu.VMEM((length, 2 * half), BF16),
                pltpu.VMEM((2 * length, half), BF16),
                pltpu.VMEM((2 * length, half), BF16),
                pltpu.VMEM(block, BF16),
                pltpu.VMEM(block, BF16),
                pltpu.VMEM(block, F32),
                pltpu.VMEM(block, F32),
                pltpu.VMEM((length, 2 * half), BF16),
                pltpu.VMEM((length, 2 * half), BF16),
                pltpu.SemaphoreType.DMA((copies,)),
                pltpu.SemaphoreType.DMA((copies,)),
                pltpu.SemaphoreType.DMA((taps.shape[0] + 8,)),
            ],
            compiler_params=pltpu.CompilerParams(
                collective_id=0, has_side_effects=True, vmem_limit_bytes=56 * 2**20),
            cost_estimate=pl.CostEstimate(
                flops=24 * length * half * half, bytes_accessed=16 * length * half, transcendentals=length * half),
        )(top, grad, taps, out_w, mix_w, rc_perm.reshape(1, half))

    return jax.shard_map(
        lambda *args: tuple(shards(*args)),
        mesh=mesh,
        in_specs=(
            P("head", "strand", "seq", None),
            P(None, "strand", "seq", "head"),
            P(None, "seq", None),
            P("seq", None),
            P("seq", None),
            P(),
        ),
        out_specs=(P("head", "strand", "seq", None), P("head", "strand", "seq", None)),
        check_vma=False,
    )
```

```python
import functools
import math

import jax
import jax.numpy as jnp
from jax import lax
from jax.experimental import pallas as pl
from jax.experimental.pallas import tpu as pltpu
from jax.sharding import PartitionSpec as P

MESH = pl.DeviceIdType.MESH
F32, BF16 = jnp.float32, jnp.bfloat16
ROUTES = ("far", "strand", "head", "head", "head")
PARTS = (1, 1, 2, 2, 2)
PIECES = [(m, k) for m in range(5) for k in range(PARTS[m])]
AHEAD = 2
LATE = True


def dot(a, b):
    return jnp.dot(a, b, preferred_element_type=F32)


def dot_t(a, b):
    return lax.dot_general(a, b, (((1,), (1,)), ((), ())), preferred_element_type=F32)


def kernel(
    n, heads, relay,
    top, grad, taps, out_w, mix_w, perm,
    restored, grad_in,
    full, onehot, topv, other, paired, cot, pad, padc, backed, back_in, pre, pulled,
    send, recv, local,
):
    s, x, z = lax.axis_index("seq"), lax.axis_index("strand"), lax.axis_index("head")
    length, half = other.shape
    dil = length // 2
    rows, width = mix_w.shape[0], grad.shape[3]
    started, counter, waits = [], [0], [0]

    def remote(src, dst, device):
        i = counter[0]
        counter[0] += 1
        return lambda s_ref=src, d_ref=dst: pltpu.make_async_remote_copy(
            src_ref=s_ref, dst_ref=d_ref, send_sem=send.at[i], recv_sem=recv.at[i],
            device_id=device, device_id_type=MESH)

    def start(make):
        copy = make()
        copy.start()
        started.append(copy)

    def arrived(make, ref):
        make(ref, ref).wait_recv()

    def here(src, dst):
        copy = pltpu.make_async_copy(src, dst, local.at[waits[0]])
        waits[0] += 1
        copy.start()
        return copy

    weights = [mix_w, out_w] + [taps.at[k] for k in range(taps.shape[0])]
    count = len(weights)
    top_copy = here(top.at[0, 0], topv)
    own_z = here(grad.at[z, 0], cot.at[:, pl.ds(pl.multiple_of(z * width, 128), width)])
    if relay:
        base = pl.multiple_of(s * rows, 16)
        own_w = [here(w, full.at[m, pl.ds(base, rows), :]) for m, w in enumerate(weights)]
    else:
        own_w = [here(w, full.at[m]) for m, w in enumerate(weights)]

    barrier = pltpu.get_barrier_semaphore()
    ring = range(1, n) if relay else ((1, n - 1) if n > 2 else range(1, n))
    greeted = [{"seq": lax.rem(s + i, n)} for i in ring]
    greeted += [{"strand": 1 - x}] + [{"head": lax.rem(z + i, heads)} for i in range(1, heads)]
    for device in greeted:
        pl.semaphore_signal(barrier, inc=1, device_id=device, device_id_type=MESH)
    pl.semaphore_wait(barrier, len(greeted))

    to_strand = {"strand": 1 - x}
    swap = remote(top.at[0, 0, :, pl.ds(0, half)], other, to_strand)
    start(swap)

    if relay:
        core = lax.rem(s, 2)
        sib, far = s + 1 - 2 * core, lax.rem(s + 2, n)
        sib_far = lax.rem(sib + 2, n)
        def seg(m, owner, first, size):
            return full.at[m, pl.ds(pl.multiple_of(owner * rows + first, 16), size), :]

        plans = []
        for m, k in PIECES:
            unit = rows // PARTS[m]
            hr = unit // 2
            turn = {"far": None, "strand": x, "head": lax.rem(z, 2)}[ROUTES[m]]
            first, size = (k * unit, unit) if turn is None else (k * unit + turn * hr, hr)
            other_half = None if turn is None else k * unit + (1 - turn) * hr
            partner = {"far": None, "strand": to_strand, "head": {"head": z + 1 - 2 * lax.rem(z, 2)}}[ROUTES[m]]
            w = weights[m]
            plan = {
                "first": first, "size": size, "rest": other_half, "hr": hr, "unit": unit,
                "sib": remote(w.at[pl.ds(k * unit, unit), :], seg(m, s, k * unit, unit), {"seq": sib}),
                "far": remote(w.at[pl.ds(first, size), :], seg(m, s, first, size), {"seq": far}),
                "fwd": remote(seg(m, far, first, size), seg(m, far, first, size), {"seq": sib}),
            }
            if turn is not None:
                plan["relay"] = remote(seg(m, far, first, size), seg(m, far, first, size), partner)
                plan["fwd2"] = remote(seg(m, far, other_half, hr), seg(m, far, other_half, hr), {"seq": sib})
            plans.append(plan)

    def push(i):
        if relay and i < len(PIECES):
            start(plans[i]["far"])
            start(plans[i]["sib"])

    def piece_a(i):
        if relay:
            p, m = plans[i], PIECES[i][0]
            arrived(p["far"], seg(m, far, p["first"], p["size"]))
            push(i + AHEAD)
            if p["rest"] is not None:
                start(p["relay"])
            start(p["fwd"])

    def piece_b(i):
        if relay and plans[i]["rest"] is not None:
            p, m = plans[i], PIECES[i][0]
            arrived(p["relay"], seg(m, far, p["rest"], p["hr"]))
            start(p["fwd2"])

    def piece_c(i):
        m, k = PIECES[i]
        if k == 0:
            own_w[m].wait()
        if relay:
            p = plans[i]
            arrived(p["sib"], seg(m, sib, k * p["unit"], p["unit"]))
            arrived(p["fwd"], seg(m, sib_far, p["first"], p["size"]))
            if p["rest"] is not None:
                arrived(p["fwd2"], seg(m, sib_far, p["rest"], p["hr"]))

    def each(stage, m):
        for i, (owner, _) in enumerate(PIECES):
            if owner == m:
                stage(i)

    stage_a = functools.partial(each, piece_a)
    stage_b = functools.partial(each, piece_b)
    stage_c = functools.partial(each, piece_c)

    def piece(h, owner):
        return cot.at[pl.ds(h * dil, dil), pl.ds(pl.multiple_of(owner * width, 128), width)]

    gifts = []
    for h in range(2):
        gifts.append([
            remote(grad.at[lax.rem(z + i, heads), 0, pl.ds(h * dil, dil), :], piece(h, z),
                   {"head": lax.rem(z + i, heads)})
            for i in range(1, heads)])
    push(0)
    for make in gifts[0]:
        start(make)
    for i in range(1, AHEAD):
        push(i)
    if not LATE:
        for make in gifts[1]:
            start(make)

    index = lax.broadcasted_iota(jnp.int32, (half, half), 0)
    onehot[...] = jnp.where(index == perm[...].reshape(1, half), 1.0, 0.0).astype(BF16)

    @pl.when(s == 0)
    def _():
        pad[0:dil] = jnp.zeros((dil, half), BF16)
        padc[0:dil] = jnp.zeros((dil, half), BF16)

    @pl.when(s == n - 1)
    def _():
        pad[3 * dil:] = jnp.zeros((dil, half), BF16)
        padc[3 * dil:] = jnp.zeros((dil, half), BF16)

    top_copy.wait()
    arrived(swap, other)
    if LATE:
        for make in gifts[1]:
            start(make)
    paired[...] = (topv[:, :half].astype(F32) + dot(other[...], onehot[...])).astype(BF16)

    def halo(buf):
        up = remote(buf.at[pl.ds(2 * dil, dil)], buf.at[pl.ds(0, dil)], {"seq": lax.rem(s + 1, n)})
        down = remote(buf.at[pl.ds(dil, dil)], buf.at[pl.ds(3 * dil, dil)], {"seq": lax.rem(s + n - 1, n)})

        @pl.when(s < n - 1)
        def _():
            up().start()

        @pl.when(s > 0)
        def _():
            down().start()

        def finish():
            @pl.when(s > 0)
            def _():
                arrived(up, buf.at[pl.ds(0, dil)])
                down().wait_send()

            @pl.when(s < n - 1)
            def _():
                arrived(down, buf.at[pl.ds(3 * dil, dil)])
                up().wait_send()

        return finish

    returns = [remote(backed.at[pl.ds(h * dil, dil)], back_in.at[pl.ds(h * dil, dil)], to_strand)
               for h in range(2)]

    def back(h):
        if h == 0:
            own_z.wait()
        for i in range(1, heads):
            arrived(gifts[h][i - 1], piece(h, lax.rem(z + heads - i, heads)))
        rows_h = slice(h * dil, (h + 1) * dil)
        backed[rows_h] = dot_t(cot[rows_h, half:], full[0]).astype(BF16)
        start(returns[h])

    stage_a(0)
    stage_a(1)
    stage_b(0)
    stage_c(0)
    input_b = (topv[:, half:].astype(F32) - dot(paired[...], full[0])).astype(BF16)
    pad[dil:3 * dil] = input_b
    restored[0, 0, :, half:] = input_b
    halo_b = halo(pad)
    back(0)
    stage_a(2)
    stage_b(1)
    stage_c(1)
    halo_b()
    stage_a(3)
    stage_b(2)
    stage_c(2)
    pre[...] = dot(pad[0:2 * dil], full[2])
    stage_a(4)
    back(1)
    stage_b(3)
    stage_c(3)
    pre[...] += dot(pad[dil:3 * dil], full[3])

    for h in range(2):
        rows_h = slice(h * dil, (h + 1) * dil)
        arrived(returns[h], back_in.at[pl.ds(h * dil, dil)])
        returned = dot_t(back_in[rows_h], onehot[...])
        cot_a = (cot[rows_h, :half].astype(F32) + backed[rows_h].astype(F32) + returned).astype(BF16)
        grad_in[0, 0, rows_h, :half] = cot_a
        pulled[rows_h] = dot_t(cot_a, full[1])

    stage_b(4)
    stage_c(4)
    scale = math.sqrt(2.0 / math.pi)
    for h in range(2):
        rows_h = slice(h * dil, (h + 1) * dil)
        v = pre[rows_h] + dot(pad[(2 + h) * dil:(3 + h) * dil], full[4])
        square = v * v
        t = jnp.tanh(scale * (v + 0.044715 * (square * v)))
        cdf = 0.5 * (1.0 + t)
        slope = cdf + 0.5 * v * (1.0 - t * t) * (scale * (1.0 + 3 * 0.044715 * square))
        padc[(1 + h) * dil:(2 + h) * dil] = (pulled[rows_h] * slope).astype(BF16)
        paired[rows_h] = (v * cdf).astype(BF16)
    halo_c = halo(padc)
    restored[0, 0, :, :half] = (topv[:, :half].astype(F32) - dot(paired[...], full[1])).astype(BF16)
    total = cot[:, half:].astype(F32) + dot_t(padc[dil:3 * dil], full[3])
    low = total[:dil] + dot_t(padc[2 * dil:3 * dil], full[2])
    high = total[dil:] + dot_t(padc[dil:2 * dil], full[4])
    halo_c()
    grad_in[0, 0, :dil, half:] = (low + dot_t(padc[:dil], full[4])).astype(BF16)
    grad_in[0, 0, dil:, half:] = (high + dot_t(padc[3 * dil:], full[2])).astype(BF16)
    for copy in started:
        copy.wait_send()


def write_out(restored, grad_in, restored_out, grad_out, sem):
    copies = [
        pltpu.make_async_copy(restored, restored_out, sem.at[0]),
        pltpu.make_async_copy(grad_in, grad_out, sem.at[1]),
    ]
    for copy in copies:
        copy.start()
    for copy in copies:
        copy.wait()


def solution(mesh):
    n, heads = mesh.shape["seq"], mesh.shape["head"]

    def shards(top, grad, taps, out_w, mix_w, rc_perm):
        relay = n == 4 and heads % 2 == 0 and mix_w.shape[0] % 32 == 0
        if not relay:
            taps = lax.all_gather(taps, "seq", axis=1, tiled=True)
            out_w = lax.all_gather(out_w, "seq", axis=0, tiled=True)
            mix_w = lax.all_gather(mix_w, "seq", axis=0, tiled=True)
        length, half = top.shape[2], top.shape[3] // 2
        block = (length, half)
        copies = 1 + 5 * len(PIECES) + 2 * (heads - 1) + 6
        found = pl.pallas_call(
            functools.partial(kernel, n, heads, relay),
            out_shape=[pltpu.VMEM(top.shape, BF16)] * 2,
            in_specs=[pl.BlockSpec(memory_space=pl.ANY)] * 5 + [pl.BlockSpec(memory_space=pltpu.VMEM)],
            out_specs=[pl.BlockSpec(memory_space=pltpu.VMEM)] * 2,
            scratch_shapes=[
                pltpu.VMEM((taps.shape[0] + 2, half, half), BF16),
                pltpu.VMEM((half, half), BF16),
                pltpu.VMEM((length, 2 * half), BF16),
                pltpu.VMEM(block, BF16),
                pltpu.VMEM(block, BF16),
                pltpu.VMEM((length, 2 * half), BF16),
                pltpu.VMEM((2 * length, half), BF16),
                pltpu.VMEM((2 * length, half), BF16),
                pltpu.VMEM(block, BF16),
                pltpu.VMEM(block, BF16),
                pltpu.VMEM(block, F32),
                pltpu.VMEM(block, F32),
                pltpu.SemaphoreType.DMA((copies,)),
                pltpu.SemaphoreType.DMA((copies,)),
                pltpu.SemaphoreType.DMA((taps.shape[0] + 8,)),
            ],
            compiler_params=pltpu.CompilerParams(
                collective_id=0, has_side_effects=True, vmem_limit_bytes=56 * 2**20),
            cost_estimate=pl.CostEstimate(
                flops=24 * length * half * half, bytes_accessed=16 * length * half, transcendentals=length * half),
        )(top, grad, taps, out_w, mix_w, rc_perm)
        return pl.pallas_call(
            write_out,
            out_shape=[jax.ShapeDtypeStruct(top.shape, BF16)] * 2,
            in_specs=[pl.BlockSpec(memory_space=pltpu.VMEM)] * 2,
            out_specs=[pl.BlockSpec(memory_space=pl.ANY)] * 2,
            scratch_shapes=[pltpu.SemaphoreType.DMA((2,))],
        )(*[pltpu.with_memory_space_constraint(f, pltpu.VMEM) for f in found])

    return jax.shard_map(
        lambda *args: tuple(shards(*args)),
        mesh=mesh,
        in_specs=(
            P("head", "strand", "seq", None),
            P(None, "strand", "seq", "head"),
            P(None, "seq", None),
            P("seq", None),
            P("seq", None),
            P(),
        ),
        out_specs=(P("head", "strand", "seq", None), P("head", "strand", "seq", None)),
        check_vma=False,
    )
```

```python
import functools
import math

import jax
import jax.numpy as jnp
from jax import lax
from jax.experimental import pallas as pl
from jax.experimental.pallas import tpu as pltpu
from jax.sharding import PartitionSpec as P

MESH = pl.DeviceIdType.MESH
F32, BF16 = jnp.float32, jnp.bfloat16
ROUTES = ('far', 'head', 'strand', 'head', 'head')
PARTS = (1, 1, 1, 1, 1)
ORDER = (0, 2, 3, 4, 1)
PIECES = [(m, k) for m in ORDER for k in range(PARTS[m])]
AHEAD = 2
LATE = True


def dot(a, b):
    return jnp.dot(a, b, preferred_element_type=F32)


def dot_t(a, b):
    return lax.dot_general(a, b, (((1,), (1,)), ((), ())), preferred_element_type=F32)


def kernel(
    n, heads, relay,
    top, grad, taps, out_w, mix_w, perm,
    restored, grad_in,
    full, onehot, topv, other, paired, cot, pad, padc, backed, back_in, pre, slope,
    send, recv, local,
):
    s, x, z = lax.axis_index("seq"), lax.axis_index("strand"), lax.axis_index("head")
    length, half = other.shape
    dil = length // 2
    rows, width = mix_w.shape[0], grad.shape[3]
    started, counter, waits = [], [0], [0]

    def remote(src, dst, device):
        i = counter[0]
        counter[0] += 1
        return lambda s_ref=src, d_ref=dst: pltpu.make_async_remote_copy(
            src_ref=s_ref, dst_ref=d_ref, send_sem=send.at[i], recv_sem=recv.at[i],
            device_id=device, device_id_type=MESH)

    def start(make):
        copy = make()
        copy.start()
        started.append(copy)

    def arrived(make, ref):
        make(ref, ref).wait_recv()

    def here(src, dst):
        copy = pltpu.make_async_copy(src, dst, local.at[waits[0]])
        waits[0] += 1
        copy.start()
        return copy

    weights = [mix_w, out_w] + [taps.at[k] for k in range(taps.shape[0])]
    count = len(weights)
    top_copy = here(top.at[0, 0], topv)
    own_z = here(grad.at[z, 0], cot.at[:, pl.ds(pl.multiple_of(z * width, 128), width)])
    if relay:
        base = pl.multiple_of(s * rows, 16)
        own_w = [here(w, full.at[m, pl.ds(base, rows), :]) for m, w in enumerate(weights)]
    else:
        own_w = [here(w, full.at[m]) for m, w in enumerate(weights)]

    barrier = pltpu.get_barrier_semaphore()
    ring = range(1, n) if relay else ((1, n - 1) if n > 2 else range(1, n))
    greeted = [{"seq": lax.rem(s + i, n)} for i in ring]
    greeted += [{"strand": 1 - x}] + [{"head": lax.rem(z + i, heads)} for i in range(1, heads)]
    for device in greeted:
        pl.semaphore_signal(barrier, inc=1, device_id=device, device_id_type=MESH)
    pl.semaphore_wait(barrier, len(greeted))

    to_strand = {"strand": 1 - x}
    swap = remote(top.at[0, 0, :, pl.ds(0, half)], other, to_strand)
    start(swap)

    if relay:
        core = lax.rem(s, 2)
        sib, far = s + 1 - 2 * core, lax.rem(s + 2, n)
        sib_far = lax.rem(sib + 2, n)
        def seg(m, owner, first, size):
            return full.at[m, pl.ds(pl.multiple_of(owner * rows + first, 16), size), :]

        plans = []
        for m, k in PIECES:
            unit = rows // PARTS[m]
            hr = unit // 2
            turn = {"far": None, "strand": x, "head": lax.rem(z, 2)}[ROUTES[m]]
            first, size = (k * unit, unit) if turn is None else (k * unit + turn * hr, hr)
            other_half = None if turn is None else k * unit + (1 - turn) * hr
            partner = {"far": None, "strand": to_strand, "head": {"head": z + 1 - 2 * lax.rem(z, 2)}}[ROUTES[m]]
            w = weights[m]
            plan = {
                "first": first, "size": size, "rest": other_half, "hr": hr, "unit": unit,
                "sib": remote(w.at[pl.ds(k * unit, unit), :], seg(m, s, k * unit, unit), {"seq": sib}),
                "far": remote(w.at[pl.ds(first, size), :], seg(m, s, first, size), {"seq": far}),
                "fwd": remote(seg(m, far, first, size), seg(m, far, first, size), {"seq": sib}),
            }
            if turn is not None:
                plan["relay"] = remote(seg(m, far, first, size), seg(m, far, first, size), partner)
                plan["fwd2"] = remote(seg(m, far, other_half, hr), seg(m, far, other_half, hr), {"seq": sib})
            plans.append(plan)

    def push(i):
        if relay and i < len(PIECES):
            start(plans[i]["far"])

    def piece_a(i):
        if relay:
            p, m = plans[i], PIECES[i][0]
            arrived(p["far"], seg(m, far, p["first"], p["size"]))
            push(i + AHEAD)
            if p["rest"] is not None:
                start(p["relay"])
            start(p["fwd"])

    def piece_b(i):
        if relay and plans[i]["rest"] is not None:
            p, m = plans[i], PIECES[i][0]
            arrived(p["relay"], seg(m, far, p["rest"], p["hr"]))
            start(p["fwd2"])

    def piece_near(i):
        m, k = PIECES[i]
        if k == 0:
            own_w[m].wait()
        if relay:
            p = plans[i]
            arrived(p["sib"], seg(m, sib, k * p["unit"], p["unit"]))

    def piece_c(i):
        m, k = PIECES[i]
        if relay:
            p = plans[i]
            arrived(p["fwd"], seg(m, sib_far, p["first"], p["size"]))
            if p["rest"] is not None:
                arrived(p["fwd2"], seg(m, sib_far, p["rest"], p["hr"]))

    def each(stage, m):
        for i, (owner, _) in enumerate(PIECES):
            if owner == m:
                stage(i)

    stage_a = functools.partial(each, piece_a)
    stage_b = functools.partial(each, piece_b)
    stage_near = functools.partial(each, piece_near)
    stage_far = functools.partial(each, piece_c)

    def stage_c(m):
        stage_near(m)
        stage_far(m)

    def piece(h, owner):
        return cot.at[pl.ds(h * dil, dil), pl.ds(pl.multiple_of(owner * width, 128), width)]

    gifts = []
    for h in range(2):
        gifts.append([
            remote(grad.at[lax.rem(z + i, heads), 0, pl.ds(h * dil, dil), :], piece(h, z),
                   {"head": lax.rem(z + i, heads)})
            for i in range(1, heads)])
    push(0)
    for make in gifts[0]:
        start(make)
    for i in range(1, AHEAD):
        push(i)
    if relay:
        for p in plans:
            start(p["sib"])
    if not LATE:
        for make in gifts[1]:
            start(make)

    index = lax.broadcasted_iota(jnp.int32, (half, half), 0)
    onehot[...] = jnp.where(index == perm[...].reshape(1, half), 1.0, 0.0).astype(BF16)

    @pl.when(s == 0)
    def _():
        pad[0:dil] = jnp.zeros((dil, half), BF16)
        padc[0:dil] = jnp.zeros((dil, half), BF16)

    @pl.when(s == n - 1)
    def _():
        pad[3 * dil:] = jnp.zeros((dil, half), BF16)
        padc[3 * dil:] = jnp.zeros((dil, half), BF16)

    top_copy.wait()
    arrived(swap, other)
    if LATE:
        for make in gifts[1]:
            start(make)
    paired[...] = (topv[:, :half].astype(F32) + dot(other[...], onehot[...])).astype(BF16)

    def halo(buf, cols):
        def rows_at(i):
            return buf.at[pl.ds(i * dil, dil), cols]

        up = remote(rows_at(2), rows_at(0), {"seq": lax.rem(s + 1, n)})
        down = remote(rows_at(1), rows_at(3), {"seq": lax.rem(s + n - 1, n)})

        @pl.when(s < n - 1)
        def _():
            up().start()

        @pl.when(s > 0)
        def _():
            down().start()

        def finish():
            @pl.when(s > 0)
            def _():
                arrived(up, rows_at(0))
                down().wait_send()

            @pl.when(s < n - 1)
            def _():
                arrived(down, rows_at(3))
                up().wait_send()

        return finish

    returns = [remote(backed.at[pl.ds(h * dil, dil)], back_in.at[pl.ds(h * dil, dil)], to_strand)
               for h in range(2)]

    def back(h):
        if h == 0:
            own_z.wait()
        for i in range(1, heads):
            arrived(gifts[h][i - 1], piece(h, lax.rem(z + heads - i, heads)))
        rows_h = slice(h * dil, (h + 1) * dil)
        backed[rows_h] = dot_t(cot[rows_h, half:], full[0]).astype(BF16)
        start(returns[h])

    stage_a(0)
    stage_a(2)
    stage_b(0)
    stage_c(0)
    input_b = (topv[:, half:].astype(F32) - dot(paired[...], full[0])).astype(BF16)
    pad[dil:3 * dil] = input_b
    halo_b = halo(pad, pl.ds(0, half))
    restored[0, 0, :, half:] = input_b
    back(0)
    stage_a(3)
    stage_b(2)
    stage_c(2)
    halo_b()
    pre[...] = dot(pad[0:2 * dil], full[2])
    stage_a(4)
    back(1)
    stage_b(3)
    stage_c(3)
    pre[...] += dot(pad[dil:3 * dil], full[3])
    stage_b(4)
    stage_a(1)
    stage_c(4)
    scale = math.sqrt(2.0 / math.pi)
    for h in range(2):
        rows_h = slice(h * dil, (h + 1) * dil)
        v = pre[rows_h] + dot(pad[(2 + h) * dil:(3 + h) * dil], full[4])
        square = v * v
        t = jnp.tanh(scale * (v + 0.044715 * (square * v)))
        cdf = 0.5 * (1.0 + t)
        slope[rows_h] = cdf + 0.5 * v * (1.0 - t * t) * (scale * (1.0 + 3 * 0.044715 * square))
        paired[rows_h] = (v * cdf).astype(BF16)

    for h in range(2):
        rows_h = slice(h * dil, (h + 1) * dil)
        arrived(returns[h], back_in.at[pl.ds(h * dil, dil)])
        returned = dot_t(back_in[rows_h], onehot[...])
        grad_in[0, 0, rows_h, :half] = (
            cot[rows_h, :half].astype(F32) + backed[rows_h].astype(F32) + returned).astype(BF16)

    near = s // 2 if relay else 0
    parts = [pl.ds(pl.multiple_of(c * (half // 2), 128), half // 2) for c in (near, 1 - near)]

    def columns(cols):
        pulled = dot_t(grad_in[0, 0, :, :half], full[1, cols, :])
        padc[dil:3 * dil, cols] = (pulled * slope[:, cols]).astype(BF16)
        return halo(padc, cols)

    def inner(cols):
        pre[...] += dot_t(padc[dil:3 * dil, cols], full[3, :, cols])
        pre[:dil] += dot_t(padc[2 * dil:3 * dil, cols], full[2, :, cols])
        pre[dil:] += dot_t(padc[dil:2 * dil, cols], full[4, :, cols])

    def edges(cols):
        return (dot_t(padc[:dil, cols], full[4, :, cols]), dot_t(padc[3 * dil:, cols], full[2, :, cols]))

    stage_near(1)
    halo_near = columns(parts[0])
    pre[...] = cot[:, half:].astype(F32)
    inner(parts[0])
    stage_b(1)
    stage_far(1)
    halo_far = columns(parts[1])
    inner(parts[1])
    restored[0, 0, :, :half] = (topv[:, :half].astype(F32) - dot(paired[...], full[1])).astype(BF16)
    halo_near()
    halo_far()
    low, high = edges(slice(None))
    grad_in[0, 0, :dil, half:] = (pre[:dil] + low).astype(BF16)
    grad_in[0, 0, dil:, half:] = (pre[dil:] + high).astype(BF16)
    for copy in started:
        copy.wait_send()


def write_out(restored, grad_in, restored_out, grad_out, sem):
    copies = [
        pltpu.make_async_copy(restored, restored_out, sem.at[0]),
        pltpu.make_async_copy(grad_in, grad_out, sem.at[1]),
    ]
    for copy in copies:
        copy.start()
    for copy in copies:
        copy.wait()


def solution(mesh):
    n, heads = mesh.shape["seq"], mesh.shape["head"]

    def shards(top, grad, taps, out_w, mix_w, rc_perm):
        relay = n == 4 and heads % 2 == 0 and mix_w.shape[0] % 32 == 0
        if not relay:
            taps = lax.all_gather(taps, "seq", axis=1, tiled=True)
            out_w = lax.all_gather(out_w, "seq", axis=0, tiled=True)
            mix_w = lax.all_gather(mix_w, "seq", axis=0, tiled=True)
        length, half = top.shape[2], top.shape[3] // 2
        block = (length, half)
        copies = 1 + 5 * len(PIECES) + 2 * (heads - 1) + 8
        found = pl.pallas_call(
            functools.partial(kernel, n, heads, relay),
            out_shape=[pltpu.VMEM(top.shape, BF16)] * 2,
            in_specs=[pl.BlockSpec(memory_space=pl.ANY)] * 5 + [pl.BlockSpec(memory_space=pltpu.VMEM)],
            out_specs=[pl.BlockSpec(memory_space=pltpu.VMEM)] * 2,
            scratch_shapes=[
                pltpu.VMEM((taps.shape[0] + 2, half, half), BF16),
                pltpu.VMEM((half, half), BF16),
                pltpu.VMEM((length, 2 * half), BF16),
                pltpu.VMEM(block, BF16),
                pltpu.VMEM(block, BF16),
                pltpu.VMEM((length, 2 * half), BF16),
                pltpu.VMEM((2 * length, half), BF16),
                pltpu.VMEM((2 * length, half), BF16),
                pltpu.VMEM(block, BF16),
                pltpu.VMEM(block, BF16),
                pltpu.VMEM(block, F32),
                pltpu.VMEM(block, F32),
                pltpu.SemaphoreType.DMA((copies,)),
                pltpu.SemaphoreType.DMA((copies,)),
                pltpu.SemaphoreType.DMA((taps.shape[0] + 8,)),
            ],
            compiler_params=pltpu.CompilerParams(
                collective_id=0, has_side_effects=True, vmem_limit_bytes=56 * 2**20),
            cost_estimate=pl.CostEstimate(
                flops=24 * length * half * half, bytes_accessed=16 * length * half, transcendentals=length * half),
        )(top, grad, taps, out_w, mix_w, rc_perm)
        return pl.pallas_call(
            write_out,
            out_shape=[jax.ShapeDtypeStruct(top.shape, BF16)] * 2,
            in_specs=[pl.BlockSpec(memory_space=pltpu.VMEM)] * 2,
            out_specs=[pl.BlockSpec(memory_space=pl.ANY)] * 2,
            scratch_shapes=[pltpu.SemaphoreType.DMA((2,))],
        )(*[pltpu.with_memory_space_constraint(f, pltpu.VMEM) for f in found])

    return jax.shard_map(
        lambda *args: tuple(shards(*args)),
        mesh=mesh,
        in_specs=(
            P("head", "strand", "seq", None),
            P(None, "strand", "seq", "head"),
            P(None, "seq", None),
            P("seq", None),
            P("seq", None),
            P(),
        ),
        out_specs=(P("head", "strand", "seq", None), P("head", "strand", "seq", None)),
        check_vma=False,
    )
```
